32 devices in a mesh: leaf: 8 (over z, y), layer: 4 (over x, core).
Axes of the slice: x: 2, y: 2, z: 4, core: 2. Of those that a mesh axis runs over, the one named last changes fastest.
Arguments:
- schur_blocks: float32 [8, 2048, 2048], P('leaf', 'layer'), as said below
Outputs:
- merged: float32 [8, 1536, 3072], P('leaf', 'layer')
- cousin_sum: float32 [8, 512, 512], P('leaf', 'layer')
Inputs may be any that keep to these rules, and one draw needn't show every extreme that they name: `schur_blocks`: symmetric and positive definite.
All inputs are finite; a program needn't handle non-finite values.
Results may differ from the reference program's by a relative error of at most 0.0001.
Values sent between devices are 32-bit elements; how exact they have to be, the bound alone decides.
A program may use at most 64 MiB of HBM per device.

```python
import math
import jax
import jax.numpy as jnp
import numpy as np
from jax import lax

IFACE = 2048
SHARED = 512
LEAVES = 8
PS = 128
OUTER = 1536
OS = 384
SHS = 128
N_LAYER = 4


def draw_schur_blocks(key, part):
    neighbours = 64.0
    reach = (neighbours / (2.0 * math.pi * IFACE)) ** 0.5
    strength = 24.0 / neighbours
    spread = 0.3

    def one_leaf(leaf_index):
        leaf_key = jax.random.fold_in(key, leaf_index)
        place_key = jax.random.fold_in(leaf_key, 21)
        noise_key = jax.random.fold_in(leaf_key, 22)
        shift_key = jax.random.fold_in(leaf_key, 23)
        places = jax.random.uniform(place_key, (IFACE, 2), jnp.float32)
        delta_x = places[:, None, 0] - places[None, :, 0]
        delta_y = places[:, None, 1] - places[None, :, 1]
        distance = jnp.sqrt(delta_x * delta_x + delta_y * delta_y)
        kernel = strength * jnp.exp(-distance / reach)
        rough = jnp.clip(jax.random.normal(noise_key, (IFACE, IFACE), jnp.float32), -6.0, 6.0)
        rough = rough * (spread / (2.0 * IFACE) ** 0.5)
        symmetric = rough + rough.T
        eye_mask = jnp.eye(IFACE, dtype=jnp.float32)
        shift = jax.random.uniform(shift_key, (IFACE,), jnp.float32, 1.0, 2.0)
        matrix = kernel + symmetric * (1.0 - eye_mask) + shift[:, None] * eye_mask
        return matrix
    return lax.map(one_leaf, jnp.arange(LEAVES, dtype=jnp.int32))


def setup_inputs(seed: int = 0) -> dict:
    streams_of = jax.random.split(jax.random.key(seed), 2)
    return {
        "schur_blocks": draw_schur_blocks(jax.random.fold_in(streams_of[1], 71), 0),
    }


def index_lists():
    slab = IFACE // N_LAYER
    sep_rows = np.array([g * slab + j for g in range(N_LAYER) for j in range(PS)], dtype=np.int32)
    out_rows = np.array([g * slab + j for g in range(N_LAYER) for j in range(PS, slab)], dtype=np.int32)
    shared_pos = np.array([g * OS + j for g in range(N_LAYER) for j in range(SHS)], dtype=np.int32)
    return (sep_rows, out_rows, shared_pos)

def reference(schur_blocks):
    sep_rows, out_rows, shared_pos = index_lists()
    highest = lax.Precision.HIGHEST

    def condense(pair):
        first = pair[0]
        second = pair[1]
        sepmat = first[sep_rows][:, sep_rows] + second[sep_rows][:, sep_rows]
        lower = jnp.linalg.cholesky(sepmat)
        factors = []
        for member in (first, second):
            coupling = member[out_rows][:, sep_rows]
            factors.append(lax.linalg.triangular_solve(lower, coupling.T, left_side=True, lower=True))
        joined = jnp.concatenate(factors, axis=1)
        blocks = []
        zeros_block = jnp.zeros((OUTER, OUTER), jnp.float32)
        for member_idx, member in enumerate((first, second)):
            direct = member[out_rows][:, out_rows]
            parts = [direct, zeros_block] if member_idx == 0 else [zeros_block, direct]
            product = jnp.dot(factors[member_idx].T.astype(jnp.float32), joined.astype(jnp.float32), precision=highest, preferred_element_type=jnp.float32)
            blocks.append(jnp.concatenate(parts, axis=1) - product)
        return jnp.stack(blocks)
    pairs = schur_blocks.reshape(LEAVES // 2, 2, IFACE, IFACE)
    merged = lax.map(condense, pairs).reshape(LEAVES, OUTER, 2 * OUTER)
    grouped = merged.reshape(LEAVES // 2, 2, OUTER, 2, OUTER)
    own_block = jnp.stack([grouped[:, 0, :, 0, :], grouped[:, 1, :, 1, :]], axis=1).reshape(LEAVES, OUTER, OUTER)
    picked = own_block[:, shared_pos][:, :, shared_pos]
    quads = picked.reshape(LEAVES // 4, 2, 2, SHARED, SHARED)
    cousin_sum = (quads + quads[:, ::-1]).reshape(LEAVES, SHARED, SHARED)
    return (merged, cousin_sum)
```

```python
import functools

import jax
import jax.numpy as jnp
from jax import lax
from jax.experimental import pallas as pl
from jax.experimental.pallas import tpu as pltpu
from jax.sharding import PartitionSpec as P

MESH = pl.DeviceIdType.MESH
F32 = jnp.float32
BF16 = jnp.bfloat16
W = 8
CORE, ACROSS, SIBLING = 1, 2, 4


def dot32(a, b, dims=((1,), (0,))):
    return lax.dot_general(
        a, b, (dims, ((), ())), precision=lax.Precision.HIGHEST, preferred_element_type=F32
    )


def split(a):
    high = a.astype(BF16)
    low = (a - high.astype(F32)).astype(BF16)
    return high, low


def invert_block(a_ref):
    n = a_ref.shape[0]
    lane = lax.broadcasted_iota(jnp.int32, (W, n), 1)
    row = lax.broadcasted_iota(jnp.int32, (W, n), 0)
    lane_all = lax.broadcasted_iota(jnp.int32, (n, n), 1)

    def panel(p, carry):
        rows = pl.ds(pl.multiple_of(p * W, W), W)
        strip = a_ref[rows, :]
        cols = [jnp.broadcast_to(strip[:, j : j + 1], (W, n)) for j in range(W)]
        rest = jnp.where(lane < W, jnp.where(lane == row, 1.0, 0.0), strip)
        for k in range(W):
            inv = 1.0 / jnp.broadcast_to(cols[k][k : k + 1, :], (W, n))
            pivot = row == k
            weight = cols[k]

            def clear(v):
                scaled = jnp.broadcast_to(v[k : k + 1, :], (W, n)) * inv
                return jnp.where(pivot, scaled, v - weight * scaled)

            rest = clear(rest)
            for j in range(k + 1, W):
                cols[j] = clear(cols[j])
        whole = a_ref[...]
        update = jnp.where(lane_all < W, 0.0, whole)
        for j in range(W):
            update = update - whole[:, j : j + 1] * rest[j : j + 1, :]
        a_ref[...] = pltpu.roll(update, n - W, 1)
        a_ref[rows, :] = pltpu.roll(rest, n - W, 1)
        return carry

    lax.fori_loop(0, n // W, panel, 0)


def gather_kernel(
    layers, a_ref, blocks_ref, y_ref, shared_ref,
    sep, mat, diag, mine, near, direct, send_sem, recv_sem, local_sem,
):
    leaf = lax.axis_index("leaf")
    layer = lax.axis_index("layer")
    core = lax.rem(layer, 2)
    slab = a_ref.shape[0]
    ps = sep.shape[1]
    outer = slab - ps
    sh = shared_ref.shape[0]
    chunks = outer // ps

    def flip(value, bit):
        return value + bit - 2 * bit * lax.rem(value // bit, 2)

    targets = {
        CORE: (leaf, flip(layer, 1)),
        ACROSS: (leaf, flip(layer, 2)),
        SIBLING: (flip(leaf, 1), layer),
    }
    corner = (
        jnp.where(core == 0, flip(leaf, 1), leaf),
        jnp.where(core == 0, layer, flip(layer, 2)),
    )

    barrier = pltpu.get_barrier_semaphore()
    for target in targets.values():
        pl.semaphore_signal(barrier, inc=1, device_id=target, device_id_type=MESH)

    loads = []
    for h in range(layers):
        cols = pl.ds(h * slab, ps)
        into = pl.ds(h * ps, ps)
        loads.append(pltpu.make_async_copy(
            a_ref.at[pl.ds(0, ps), cols], sep.at[0, :, into], local_sem.at[h]))
    for h in range(layers):
        cols = pl.ds(h * slab, ps)
        into = pl.ds(h * ps, ps)
        loads.append(pltpu.make_async_copy(
            a_ref.at[pl.ds(ps, outer), cols], mine.at[:, into], local_sem.at[layers + h]))
    for h in range(layers):
        loads.append(pltpu.make_async_copy(
            a_ref.at[pl.ds(ps, sh), pl.ds(h * slab + ps, sh)],
            direct.at[:, pl.ds(h * sh, sh)], local_sem.at[2 * layers + h]))
    for load in loads:
        load.start()

    def place(slot, q):
        if q == 0:
            return sep.at[slot]
        return blocks_ref.at[slot, pl.ds((q - 1) * ps, ps), :]

    def origin(slot, q):
        if q > 0 and isinstance(slot, int) and slot == 0:
            return mine.at[pl.ds((q - 1) * ps, ps), :]
        return place(slot, q)

    sources = {1: 0, 2: 0, 4: 0, 3: 2, 5: 4, 6: 2 + 2 * core, 7: 6}
    ways = {1: CORE, 2: ACROSS, 4: SIBLING, 3: CORE, 5: CORE, 7: CORE}

    def transfer(slot, q):
        return pltpu.make_async_remote_copy(
            src_ref=origin(sources[slot], q),
            dst_ref=place(slot, q),
            send_sem=send_sem.at[slot, q],
            recv_sem=recv_sem.at[slot, q],
            device_id=corner if slot == 6 else targets[ways[slot]],
            device_id_type=MESH,
        )

    def first(q):
        for slot in (SIBLING, ACROSS, CORE):
            transfer(slot, q).start()

    def second(q):
        transfer(2, q).wait_recv()
        transfer(4, q).wait_recv()
        transfer(6, q).start()
        transfer(3, q).start()
        transfer(5, q).start()

    def third(q):
        transfer(6, q).wait_recv()
        transfer(7, q).start()

    def last(q):
        for slot in (1, 3, 5, 7):
            transfer(slot, q).wait_recv()

    for load in loads[:layers]:
        load.wait()
    pl.semaphore_wait(barrier, 3)
    first(0)
    for load in loads[layers:]:
        load.wait()
    keep = pltpu.make_async_copy(mine, blocks_ref.at[0], local_sem.at[3 * layers])
    keep.start()
    second(0)
    first(1)
    third(0)
    for q in range(2, chunks + 1):
        first(q)
    last(0)

    for r in range(layers):
        h = layer + r - 2 * (
            lax.rem(layer, 2) * (r % 2) + 2 * lax.rem(layer // 2, 2) * (r // 2)
        )
        mat[pl.ds(pl.multiple_of(h * ps, ps), ps), :] = sep[r] + sep[r + SIBLING]

    for b in range(layers):
        mid = slice(b * ps, (b + 1) * ps)
        diag[...] = mat[mid, mid]
        invert_block(diag)
        turned = dot32(diag[...], mat[mid, :])
        mat[mid, :] = turned
        mat[mid, mid] = diag[...]
        turned = mat[mid, :]
        for other in range(layers):
            if other == b:
                continue
            rows = slice(other * ps, (other + 1) * ps)
            weight = mat[rows, mid]
            mat[rows, mid] = jnp.zeros((ps, ps), F32)
            mat[rows, :] = mat[rows, :] - dot32(weight, turned)
        if b + 1 <= chunks:
            second(b + 1)
        if 1 <= b <= chunks:
            third(b)
    for q in range(layers, chunks + 1):
        third(q)
    last(1)
    fetch = [
        pltpu.make_async_copy(blocks_ref.at[r, pl.ds(0, sh), :], near.at[r - 1], local_sem.at[r])
        for r in range(1, layers)
    ]
    for copy in fetch:
        copy.start()
    y_ref[...] = dot32(mine[...], mat[...])
    for copy in fetch:
        copy.wait()
    for r in range(layers):
        h = layer + r - 2 * (
            lax.rem(layer, 2) * (r % 2) + 2 * lax.rem(layer // 2, 2) * (r // 2)
        )
        cols = pl.ds(pl.multiple_of(h * sh, sh), sh)
        far = mine[0:sh, :] if r == 0 else near[r - 1]
        shared_ref[:, cols] = direct[:, cols] - dot32(y_ref[0:sh, :], far, ((1,), (1,)))
    keep.wait()
    for q in range(2, chunks + 1):
        last(q)
    for q in range(chunks + 1):
        for slot in range(1, 8):
            transfer(slot, q).wait_send()


def merge_kernel(layers, where_ref, y_ref, block_ref, a_ref, out_ref, wide):
    r = pl.program_id(0)
    depth = y_ref.shape[1]
    ps = a_ref.shape[0] - out_ref.shape[0]

    @pl.when(r == 0)
    def _():
        high, low = split(y_ref[...])
        wide[:, 0:depth] = high
        wide[:, depth : 2 * depth] = high
        wide[:, 2 * depth : 3 * depth] = low

    high, low = split(block_ref[0])
    far = jnp.concatenate([high, low, high], axis=1)
    product = lax.dot_general(
        wide[...], far, (((1,), (1,)), ((), ())), preferred_element_type=F32
    )

    @pl.when(r < layers)
    def _():
        out_ref[...] = a_ref[ps:, ps:] - product

    @pl.when(r >= layers)
    def _():
        out_ref[...] = 0.0 - product


def on_device(layers, schur_blocks):
    local = schur_blocks[0]
    slab, width = local.shape
    ps = slab // 4
    depth = layers * ps
    outer = slab - ps
    sh = ps
    group = 2 * layers
    chunks = outer // ps
    blocks, y, own = pl.pallas_call(
        functools.partial(gather_kernel, layers),
        out_shape=(
            jax.ShapeDtypeStruct((group, outer, depth), F32),
            jax.ShapeDtypeStruct((outer, depth), F32),
            jax.ShapeDtypeStruct((sh, layers * sh), F32),
        ),
        in_specs=[pl.BlockSpec(memory_space=pl.ANY)],
        out_specs=(
            pl.BlockSpec(memory_space=pl.ANY),
            pl.BlockSpec(memory_space=pltpu.VMEM),
            pl.BlockSpec(memory_space=pltpu.VMEM),
        ),
        scratch_shapes=[
            pltpu.VMEM((group, ps, depth), F32),
            pltpu.VMEM((depth, depth), F32),
            pltpu.VMEM((ps, ps), F32),
            pltpu.VMEM((outer, depth), F32),
            pltpu.VMEM((layers - 1, sh, depth), F32),
            pltpu.VMEM((sh, layers * sh), F32),
            pltpu.SemaphoreType.DMA((group, chunks + 1)),
            pltpu.SemaphoreType.DMA((group, chunks + 1)),
            pltpu.SemaphoreType.DMA((3 * layers + 1,)),
        ],
        compiler_params=pltpu.CompilerParams(
            collective_id=0, has_side_effects=True, vmem_limit_bytes=40 * 2**20
        ),
    )(local)

    leaf = lax.axis_index("leaf")
    layer = lax.axis_index("layer")
    me = (leaf % 2) * layers + layer
    order = jnp.bitwise_xor(me, jnp.arange(group, dtype=jnp.int32))
    slabs = jnp.bitwise_xor(layer, jnp.minimum(jnp.arange(group, dtype=jnp.int32), layers - 1))
    where = jnp.concatenate([order, slabs]).astype(jnp.int32)
    merged = pl.pallas_call(
        functools.partial(merge_kernel, layers),
        out_shape=jax.ShapeDtypeStruct((outer, group * outer), F32),
        grid_spec=pltpu.PrefetchScalarGridSpec(
            num_scalar_prefetch=1,
            grid=(group,),
            in_specs=[
                pl.BlockSpec((outer, depth), lambda r, w: (0, 0)),
                pl.BlockSpec((1, outer, depth), lambda r, w: (r, 0, 0)),
                pl.BlockSpec((slab, slab), lambda r, w: (0, w[group + r])),
            ],
            out_specs=pl.BlockSpec((outer, outer), lambda r, w: (0, w[r])),
            scratch_shapes=[pltpu.VMEM((outer, 3 * depth), BF16)],
        ),
        compiler_params=pltpu.CompilerParams(vmem_limit_bytes=40 * 2**20),
        cost_estimate=pl.CostEstimate(
            flops=6 * outer * depth * group * outer,
            bytes_accessed=4 * (group * outer * (outer + depth) + slab * width),
            transcendentals=0,
        ),
    )(where, y, blocks, local)
    count = lax.axis_size("leaf")
    cousin = lax.ppermute(own, "leaf", [(s, s ^ 2) for s in range(count)])
    return (merged[None], (own + cousin)[None])


def solution(mesh):
    placed = (P("leaf", "layer", None),)
    return jax.shard_map(
        functools.partial(on_device, mesh.shape["layer"]),
        mesh=mesh,
        in_specs=placed,
        out_specs=(P("leaf", "layer", None), P("leaf", "layer", None)),
        check_vma=False,
    )
```

```python
import functools

import jax
import jax.numpy as jnp
from jax import lax
from jax.experimental import pallas as pl
from jax.experimental.pallas import tpu as pltpu
from jax.sharding import PartitionSpec as P

MESH = pl.DeviceIdType.MESH
F32 = jnp.float32
BF16 = jnp.bfloat16
W = 8
CORE, ACROSS, SIBLING = 1, 2, 4


def dot32(a, b, dims=((1,), (0,))):
    return lax.dot_general(
        a, b, (dims, ((), ())), precision=lax.Precision.HIGHEST, preferred_element_type=F32
    )


def split(a):
    high = a.astype(BF16)
    low = (a - high.astype(F32)).astype(BF16)
    return high, low


def refine(d):
    r = pl.reciprocal(d, approx=True)
    r = r * (2.0 - d * r)
    return r * (2.0 - d * r)


def rank_update(old, pivots):
    lane = lax.broadcasted_iota(jnp.int32, old.shape, 1)
    terms = [old[:, j : j + 1] * pivots[j : j + 1, :] for j in range(W)]
    while len(terms) > 1:
        terms = [terms[i] + terms[i + 1] for i in range(0, len(terms), 2)]
    return jnp.where(lane < W, 0.0, old) - terms[0]


def pivot_rows(strip, first):
    n = strip.shape[1]
    lane = lax.broadcasted_iota(jnp.int32, (W, n), 1)
    row = lax.broadcasted_iota(jnp.int32, (W, n), 0)
    cols = [jnp.broadcast_to(strip[:, first + j : first + j + 1], (W, n)) for j in range(W)]
    turned = pltpu.roll(strip, n - first, 1) if first else strip
    rest = jnp.where(lane < W, jnp.where(lane == row, 1.0, 0.0), turned)
    for k in range(W):
        inv = refine(jnp.broadcast_to(cols[k][k : k + 1, :], (W, n)))
        pivot = row == k
        weight = cols[k]

        def clear(v):
            head = jnp.broadcast_to(v[k : k + 1, :], (W, n))
            return jnp.where(pivot, head * inv, v - (weight * head) * inv)

        for j in range(k + 1, W):
            cols[j] = clear(cols[j])
        rest = clear(rest)
    return rest


def invert_start(a_ref):
    pivots = pivot_rows(a_ref[0:W, :], 0)
    return pivots, rank_update(a_ref[W : 2 * W, :], pivots)


def apply_rows(a_ref, p, pivots):
    n = a_ref.shape[0]
    a_ref[...] = pltpu.roll(rank_update(a_ref[...], pivots), n - W, 1)
    a_ref[pl.ds(pl.multiple_of(p * W, W), W), :] = pltpu.roll(pivots, n - W, 1)


def invert_steps(a_ref, start, stop, state):
    count = a_ref.shape[0] // W

    def panel(p, state):
        before, strip = state
        pivots = pivot_rows(strip, W)
        apply_rows(a_ref, p - 1, before)
        follow = lax.rem(p + 1, count)
        after = a_ref[pl.ds(pl.multiple_of(follow * W, W), W), :]
        return pivots, rank_update(after, pivots)

    return lax.fori_loop(start, stop, panel, state)


def gather_kernel(
    layers, a_ref, blocks_ref, y_ref, shared_ref,
    sep, lead, mat, diag, mine, near, direct, send_sem, recv_sem, local_sem,
):
    leaf = lax.axis_index("leaf")
    layer = lax.axis_index("layer")
    core = lax.rem(layer, 2)
    slab = a_ref.shape[0]
    ps = sep.shape[1]
    outer = slab - ps
    sh = shared_ref.shape[0]
    chunks = outer // ps

    def flip(value, bit):
        return value + bit - 2 * bit * lax.rem(value // bit, 2)

    targets = {
        CORE: (leaf, flip(layer, 1)),
        ACROSS: (leaf, flip(layer, 2)),
        SIBLING: (flip(leaf, 1), layer),
    }
    corner = (
        jnp.where(core == 0, flip(leaf, 1), leaf),
        jnp.where(core == 0, layer, flip(layer, 2)),
    )

    barrier = pltpu.get_barrier_semaphore()
    for target in targets.values():
        pl.semaphore_signal(barrier, inc=1, device_id=target, device_id_type=MESH)

    loads = []
    for h in range(layers):
        cols = pl.ds(h * slab, ps)
        into = pl.ds(h * ps, ps)
        loads.append(pltpu.make_async_copy(
            a_ref.at[pl.ds(0, ps), cols], sep.at[0, :, into], local_sem.at[h]))
    for h in range(layers):
        cols = pl.ds(h * slab, ps)
        into = pl.ds(h * ps, ps)
        loads.append(pltpu.make_async_copy(
            a_ref.at[pl.ds(ps, outer), cols], mine.at[:, into], local_sem.at[layers + h]))
    for h in range(layers):
        loads.append(pltpu.make_async_copy(
            a_ref.at[pl.ds(ps, sh), pl.ds(h * slab + ps, sh)],
            direct.at[:, pl.ds(h * sh, sh)], local_sem.at[2 * layers + h]))
    for load in loads:
        load.start()

    def place(slot, q):
        if q == 0:
            return sep.at[slot]
        return blocks_ref.at[slot, pl.ds((q - 1) * ps, ps), :]

    def origin(slot, q):
        if q > 0 and isinstance(slot, int) and slot == 0:
            return mine.at[pl.ds((q - 1) * ps, ps), :]
        return place(slot, q)

    sources = {1: 0, 2: 0, 4: 0, 3: 2, 5: 4, 6: 2 + 2 * core, 7: 6}
    ways = {1: CORE, 2: ACROSS, 4: SIBLING, 3: CORE, 5: CORE, 7: CORE}

    def transfer(slot, q):
        return pltpu.make_async_remote_copy(
            src_ref=origin(sources[slot], q),
            dst_ref=place(slot, q),
            send_sem=send_sem.at[slot, q],
            recv_sem=recv_sem.at[slot, q],
            device_id=corner if slot == 6 else targets[ways[slot]],
            device_id_type=MESH,
        )

    def first(q):
        for slot in (SIBLING, ACROSS, CORE):
            transfer(slot, q).start()

    def second(q):
        transfer(2, q).wait_recv()
        transfer(4, q).wait_recv()
        transfer(6, q).start()
        transfer(3, q).start()
        transfer(5, q).start()

    def third(q):
        transfer(6, q).wait_recv()
        transfer(7, q).start()

    def last(q):
        for slot in (1, 3, 5, 7):
            transfer(slot, q).wait_recv()

    def xor(r):
        return layer + r - 2 * (
            lax.rem(layer, 2) * (r % 2) + 2 * lax.rem(layer // 2, 2) * (r // 2)
        )

    def span(r):
        return pl.ds(pl.multiple_of(xor(r) * ps, ps), ps)

    for load in loads[:layers]:
        load.wait()
    pl.semaphore_wait(barrier, 3)
    ahead = pltpu.make_async_remote_copy(
        src_ref=sep.at[0, :, span(0)],
        dst_ref=lead,
        send_sem=send_sem.at[0, 0],
        recv_sem=recv_sem.at[0, 0],
        device_id=targets[SIBLING],
        device_id_type=MESH,
    )
    ahead.start()
    first(0)
    for load in loads[layers:]:
        load.wait()
    keep = pltpu.make_async_copy(mine, blocks_ref.at[0], local_sem.at[3 * layers])
    keep.start()
    ahead.wait_recv()
    half = ps // W // 2
    for b in range(layers):
        mid = span(b)
        diag[...] = sep[0, :, mid] + lead[...] if b == 0 else mat[mid, mid]
        state = invert_start(diag)
        state = invert_steps(diag, 1, half, state)
        if b == 0:
            second(0)
            first(1)
        else:
            second(b)
            if b < chunks:
                first(b + 1)
        state = invert_steps(diag, half, 2 * half, state)
        apply_rows(diag, 2 * half - 1, state[0])
        third(b)
        if b == 0:
            last(0)
            for r in range(layers):
                mat[span(r), :] = sep[r] + sep[r + SIBLING]
        mat[mid, :] = dot32(diag[...], mat[mid, :])
        mat[mid, mid] = diag[...]
        turned = mat[mid, :]
        for other in range(layers):
            if other == b:
                continue
            rows = span(other)
            weight = mat[rows, mid]
            mat[rows, mid] = jnp.zeros((ps, ps), F32)
            mat[rows, :] = mat[rows, :] - dot32(weight, turned)
    for q in range(layers, chunks + 1):
        third(q)
    last(1)
    fetch = [
        pltpu.make_async_copy(blocks_ref.at[r, pl.ds(0, sh), :], near.at[r - 1], local_sem.at[r])
        for r in range(1, layers)
    ]
    for copy in fetch:
        copy.start()
    y_ref[...] = dot32(mine[...], mat[...])
    for copy in fetch:
        copy.wait()
    for r in range(layers):
        cols = pl.ds(pl.multiple_of(xor(r) * sh, sh), sh)
        far = mine[0:sh, :] if r == 0 else near[r - 1]
        shared_ref[:, cols] = direct[:, cols] - dot32(y_ref[0:sh, :], far, ((1,), (1,)))
    keep.wait()
    for q in range(2, chunks + 1):
        last(q)
    for q in range(chunks + 1):
        for slot in range(1, 8):
            transfer(slot, q).wait_send()
    ahead.wait_send()


def merge_kernel(layers, where_ref, y_ref, block_ref, a_ref, out_ref, wide):
    r = pl.program_id(0)
    depth = y_ref.shape[1]
    ps = a_ref.shape[0] - out_ref.shape[0]

    @pl.when(r == 0)
    def _():
        high, low = split(y_ref[...])
        wide[:, 0:depth] = high
        wide[:, depth : 2 * depth] = high
        wide[:, 2 * depth : 3 * depth] = low

    outer = out_ref.shape[0]
    slab = a_ref.shape[0]
    swap = where_ref[0] % 2
    parts = []
    for i in range(2):
        high, low = split(block_ref[jnp.bitwise_xor(swap, i)])
        parts.append(jnp.concatenate([high, low, high], axis=1))
    product = lax.dot_general(
        wide[...], jnp.concatenate(parts, axis=0), (((1,), (1,)), ((), ())),
        preferred_element_type=F32,
    )

    @pl.when(r < layers // 2)
    def _():
        for i in range(2):
            cols = slice(i * outer, (i + 1) * outer)
            out_ref[:, cols] = a_ref[ps:, i * slab + ps : (i + 1) * slab] - product[:, cols]

    @pl.when(r >= layers // 2)
    def _():
        out_ref[...] = 0.0 - product


def on_device(layers, schur_blocks):
    local = schur_blocks[0]
    slab, width = local.shape
    ps = slab // 4
    depth = layers * ps
    outer = slab - ps
    sh = ps
    group = 2 * layers
    chunks = outer // ps
    blocks, y, own = pl.pallas_call(
        functools.partial(gather_kernel, layers),
        out_shape=(
            jax.ShapeDtypeStruct((group, outer, depth), F32),
            jax.ShapeDtypeStruct((outer, depth), F32),
            jax.ShapeDtypeStruct((sh, layers * sh), F32),
        ),
        in_specs=[pl.BlockSpec(memory_space=pl.ANY)],
        out_specs=(
            pl.BlockSpec(memory_space=pl.ANY),
            pl.BlockSpec(memory_space=pltpu.VMEM),
            pl.BlockSpec(memory_space=pltpu.VMEM),
        ),
        scratch_shapes=[
            pltpu.VMEM((group, ps, depth), F32),
            pltpu.VMEM((ps, ps), F32),
            pltpu.VMEM((depth, depth), F32),
            pltpu.VMEM((ps, ps), F32),
            pltpu.VMEM((outer, depth), F32),
            pltpu.VMEM((layers - 1, sh, depth), F32),
            pltpu.VMEM((sh, layers * sh), F32),
            pltpu.SemaphoreType.DMA((group, chunks + 1)),
            pltpu.SemaphoreType.DMA((group, chunks + 1)),
            pltpu.SemaphoreType.DMA((3 * layers + 1,)),
        ],
        compiler_params=pltpu.CompilerParams(
            collective_id=0, has_side_effects=True, vmem_limit_bytes=60 * 2**20
        ),
    )(local)

    leaf = lax.axis_index("leaf")
    layer = lax.axis_index("layer")
    me = (leaf % 2) * layers + layer
    where = jnp.full((1,), me, jnp.int32)
    merged = pl.pallas_call(
        functools.partial(merge_kernel, layers),
        out_shape=jax.ShapeDtypeStruct((outer, group * outer), F32),
        grid_spec=pltpu.PrefetchScalarGridSpec(
            num_scalar_prefetch=1,
            grid=(group // 2,),
            in_specs=[
                pl.BlockSpec((outer, depth), lambda r, w: (0, 0)),
                pl.BlockSpec((2, outer, depth), lambda r, w: (r, 0, 0)),
                pl.BlockSpec(
                    (slab, 2 * slab),
                    lambda r, w: (
                        0,
                        jnp.bitwise_xor(w[0] % layers // 2, jnp.minimum(r, layers // 2 - 1)),
                    ),
                ),
            ],
            out_specs=pl.BlockSpec(
                (outer, 2 * outer), lambda r, w: (0, jnp.bitwise_xor(w[0] // 2, r))
            ),
            scratch_shapes=[pltpu.VMEM((outer, 3 * depth), BF16)],
        ),
        compiler_params=pltpu.CompilerParams(vmem_limit_bytes=60 * 2**20),
        cost_estimate=pl.CostEstimate(
            flops=6 * outer * depth * group * outer,
            bytes_accessed=4 * (group * outer * (outer + depth) + slab * width),
            transcendentals=0,
        ),
    )(where, y, blocks, local)
    count = lax.axis_size("leaf")
    cousin = lax.ppermute(own, "leaf", [(s, s ^ 2) for s in range(count)])
    return (merged[None], (own + cousin)[None])


def solution(mesh):
    placed = (P("leaf", "layer", None),)
    return jax.shard_map(
        functools.partial(on_device, mesh.shape["layer"]),
        mesh=mesh,
        in_specs=placed,
        out_specs=(P("leaf", "layer", None), P("leaf", "layer", None)),
        check_vma=False,
    )
```

```python
import functools

import jax
import jax.numpy as jnp
from jax import lax
from jax.experimental import pallas as pl
from jax.experimental.pallas import tpu as pltpu
from jax.sharding import PartitionSpec as P

MESH = pl.DeviceIdType.MESH
F32 = jnp.float32
BF16 = jnp.bfloat16
W = 8
CORE, ACROSS, SIBLING = 1, 2, 4


def dot32(a, b, dims=((1,), (0,))):
    return lax.dot_general(
        a, b, (dims, ((), ())), precision=lax.Precision.HIGHEST, preferred_element_type=F32
    )


def split(a):
    high = a.astype(BF16)
    low = (a - high.astype(F32)).astype(BF16)
    return high, low


def refine(d):
    r = pl.reciprocal(d, approx=True)
    r = r * (2.0 - d * r)
    return r * (2.0 - d * r)


def rank_update(old, pivots):
    lane = lax.broadcasted_iota(jnp.int32, old.shape, 1)
    terms = [old[:, j : j + 1] * pivots[j : j + 1, :] for j in range(W)]
    while len(terms) > 1:
        terms = [terms[i] + terms[i + 1] for i in range(0, len(terms), 2)]
    return jnp.where(lane < W, 0.0, old) - terms[0]


def pivot_rows(strip, first):
    n = strip.shape[1]
    lane = lax.broadcasted_iota(jnp.int32, (W, n), 1)
    row = lax.broadcasted_iota(jnp.int32, (W, n), 0)
    cols = [jnp.broadcast_to(strip[:, first + j : first + j + 1], (W, n)) for j in range(W)]
    turned = pltpu.roll(strip, n - first, 1) if first else strip
    rest = jnp.where(lane < W, jnp.where(lane == row, 1.0, 0.0), turned)

    def spread(v, k):
        return jnp.broadcast_to(v[k : k + 1, :], (W, n))

    scale = [pl.reciprocal(spread(cols[k], k), approx=True) for k in range(W)]
    for k in range(0, W, 2):
        ua, uc = scale[k], scale[k + 1]
        a, b, c = spread(cols[k], k), spread(cols[k], k + 1), spread(cols[k + 1], k + 1)
        au, cu, bu = a * ua, c * uc, b * ua
        inv = refine(au * cu - bu * (b * uc))
        first_first, second_second, cross = cu * ua, au * uc, bu * uc
        w1, w2 = cols[k], cols[k + 1]

        def clear(v):
            v1, v2 = spread(v, k), spread(v, k + 1)
            n1 = first_first * v1 - cross * v2
            n2 = second_second * v2 - cross * v1
            q = w1 * n1 + w2 * n2
            left = jnp.where(row == k, 0.0, jnp.where(row == k + 1, 0.0, v))
            q = jnp.where(row == k, -n1, jnp.where(row == k + 1, -n2, q))
            return left - q * inv

        for j in range(k + 2, W):
            cols[j] = clear(cols[j])
        rest = clear(rest)
    return rest


def invert_start(a_ref):
    pivots = pivot_rows(a_ref[0:W, :], 0)
    return pivots, rank_update(a_ref[W : 2 * W, :], pivots)


def apply_rows(a_ref, p, pivots):
    n = a_ref.shape[0]
    turned = pltpu.roll(pivots, n - W, 1)
    lane = lax.broadcasted_iota(jnp.int32, (n - W, n), 1)
    row = lax.broadcasted_iota(jnp.int32, (n - W, n), 0)
    step = jnp.concatenate([-turned, jnp.where(lane == row, 1.0, 0.0)], axis=0)
    a_ref[...] = dot32(a_ref[...], step)
    a_ref[pl.ds(pl.multiple_of(p * W, W), W), :] = turned


def invert_steps(a_ref, start, stop, state):
    count = a_ref.shape[0] // W

    def panel(p, state):
        before, strip = state
        pivots = pivot_rows(strip, W)
        apply_rows(a_ref, p - 1, before)
        follow = lax.rem(p + 1, count)
        after = a_ref[pl.ds(pl.multiple_of(follow * W, W), W), :]
        return pivots, rank_update(after, pivots)

    return lax.fori_loop(start, stop, panel, state)


def gather_kernel(
    layers, a_ref, out_ref, shared_ref,
    sep, lead, mat, diag, mine, direct, blocks_ref, y_ref, wide, result, own, cousin, send_sem, recv_sem, local_sem,
):
    leaf = lax.axis_index("leaf")
    layer = lax.axis_index("layer")
    core = lax.rem(layer, 2)
    slab = a_ref.shape[0]
    ps = sep.shape[1]
    outer = slab - ps
    sh = shared_ref.shape[0]
    chunks = outer // ps

    def flip(value, bit):
        return value + bit - 2 * bit * lax.rem(value // bit, 2)

    targets = {
        CORE: (leaf, flip(layer, 1)),
        ACROSS: (leaf, flip(layer, 2)),
        SIBLING: (flip(leaf, 1), layer),
    }
    corner = (
        jnp.where(core == 0, flip(leaf, 1), leaf),
        jnp.where(core == 0, layer, flip(layer, 2)),
    )

    barrier = pltpu.get_barrier_semaphore()
    relative = (flip(leaf, 2), layer)
    for target in (*targets.values(), relative):
        pl.semaphore_signal(barrier, inc=1, device_id=target, device_id_type=MESH)

    loads = []
    for h in range(layers):
        cols = pl.ds(h * slab, ps)
        into = pl.ds(h * ps, ps)
        loads.append(pltpu.make_async_copy(
            a_ref.at[pl.ds(0, ps), cols], sep.at[0, :, into], local_sem.at[h]))
    for h in range(layers):
        cols = pl.ds(h * slab, ps)
        into = pl.ds(h * ps, ps)
        loads.append(pltpu.make_async_copy(
            a_ref.at[pl.ds(ps, outer), cols], mine.at[:, into], local_sem.at[layers + h]))
    for h in range(layers):
        loads.append(pltpu.make_async_copy(
            a_ref.at[pl.ds(ps, outer), pl.ds(h * slab + ps, outer)],
            direct.at[:, pl.ds(h * outer, outer)], local_sem.at[2 * layers + h]))
    for load in loads:
        load.start()

    def place(slot, q):
        if q == 0:
            return sep.at[slot]
        return blocks_ref.at[slot, pl.ds((q - 1) * ps, ps), :]

    def origin(slot, q):
        if q > 0 and isinstance(slot, int) and slot == 0:
            return mine.at[pl.ds((q - 1) * ps, ps), :]
        return place(slot, q)

    sources = {1: 0, 2: 0, 4: 0, 3: 2, 5: 4, 6: 2 + 2 * core, 7: 6}
    ways = {1: CORE, 2: ACROSS, 4: SIBLING, 3: CORE, 5: CORE, 7: CORE}

    def transfer(slot, q):
        return pltpu.make_async_remote_copy(
            src_ref=origin(sources[slot], q),
            dst_ref=place(slot, q),
            send_sem=send_sem.at[slot, q],
            recv_sem=recv_sem.at[slot, q],
            device_id=corner if slot == 6 else targets[ways[slot]],
            device_id_type=MESH,
        )

    def first(q):
        for slot in (SIBLING, ACROSS, CORE):
            transfer(slot, q).start()

    def second(q):
        transfer(2, q).wait_recv()
        transfer(4, q).wait_recv()
        transfer(6, q).start()
        transfer(3, q).start()
        transfer(5, q).start()

    def third(q):
        transfer(6, q).wait_recv()
        transfer(7, q).start()

    def last(q):
        for slot in (1, 3, 5, 7):
            transfer(slot, q).wait_recv()

    def xor(r):
        return layer + r - 2 * (
            lax.rem(layer, 2) * (r % 2) + 2 * lax.rem(layer // 2, 2) * (r // 2)
        )

    def span(r):
        return pl.ds(pl.multiple_of(xor(r) * ps, ps), ps)

    for load in loads[:layers]:
        load.wait()
    pl.semaphore_wait(barrier, 4)
    ahead = pltpu.make_async_remote_copy(
        src_ref=sep.at[0, :, span(0)],
        dst_ref=lead,
        send_sem=send_sem.at[0, 0],
        recv_sem=recv_sem.at[0, 0],
        device_id=targets[SIBLING],
        device_id_type=MESH,
    )
    ahead.start()
    first(0)
    for load in loads[layers : 2 * layers]:
        load.wait()
    keep = pltpu.make_async_copy(mine, blocks_ref.at[0], local_sem.at[3 * layers])
    keep.start()
    ahead.wait_recv()
    half = ps // W // 2
    for b in range(layers):
        mid = span(b)
        diag[...] = sep[0, :, mid] + lead[...] if b == 0 else mat[mid, mid]
        state = invert_start(diag)
        state = invert_steps(diag, 1, half, state)
        second(b)
        if b == 0:
            for q in range(1, chunks + 1):
                first(q)
        state = invert_steps(diag, half, 2 * half, state)
        apply_rows(diag, 2 * half - 1, state[0])
        third(b)
        if b == 0:
            last(0)
            for r in range(layers):
                mat[span(r), :] = sep[r] + sep[r + SIBLING]
        mat[mid, :] = dot32(diag[...], mat[mid, :])
        mat[mid, mid] = diag[...]
        turned = mat[mid, :]
        for other in range(layers):
            if other == b:
                continue
            rows = span(other)
            weight = mat[rows, mid]
            mat[rows, mid] = jnp.zeros((ps, ps), F32)
            mat[rows, :] = mat[rows, :] - dot32(weight, turned)
    for q in range(layers, chunks + 1):
        third(q)
    y_ref[...] = dot32(mine[...], mat[...])
    depth = y_ref.shape[1]
    high, low = split(y_ref[...])
    wide[:, 0:depth] = high
    wide[:, depth : 2 * depth] = high
    wide[:, 2 * depth : 3 * depth] = low
    for load in loads[2 * layers :]:
        load.wait()
    last(1)
    for r in range(layers):
        cols = pl.ds(pl.multiple_of(xor(r) * sh, sh), sh)
        from_cols = pl.ds(pl.multiple_of(xor(r) * outer, sh), sh)
        far = mine[0:sh, :] if r == 0 else blocks_ref[r, 0:sh, :]
        own[:, cols] = direct[0:sh, from_cols] - dot32(y_ref[0:sh, :], far, ((1,), (1,)))
    swap = pltpu.make_async_remote_copy(
        src_ref=own,
        dst_ref=cousin,
        send_sem=send_sem.at[0, 1],
        recv_sem=recv_sem.at[0, 1],
        device_id=relative,
        device_id_type=MESH,
    )
    swap.start()
    keep.wait()
    pair = 2 * outer
    writes = []
    for t in range(layers):
        for q in range(2, chunks + 1):
            transfer(2 * t + 1, q).wait_recv()
        near = t < layers // 2
        place_in = xor(2 * (t % (layers // 2))) // 2
        parity = lax.rem(leaf, 2)
        side = parity if near else 1 - parity
        parts = []
        for i in range(2):
            slot = 2 * t + (core if i == 0 else 1 - core)
            high, low = split(blocks_ref[slot])
            parts.append(jnp.concatenate([high, low, high], axis=1))
        product = lax.dot_general(
            wide[...], jnp.concatenate(parts, axis=0), (((1,), (1,)), ((), ())),
            preferred_element_type=F32,
        )
        if near:
            product = direct[:, pl.ds(pl.multiple_of(place_in * pair, sh), pair)] - product
        else:
            product = 0.0 - product
        result[t] = product
        to = (side * (layers // 2) + place_in) * pair
        write = pltpu.make_async_copy(
            result.at[t], out_ref.at[:, pl.ds(pl.multiple_of(to, sh), pair)], local_sem.at[t]
        )
        write.start()
        writes.append(write)
    swap.wait()
    shared_ref[...] = own[...] + cousin[...]
    for write in writes:
        write.wait()
    for q in range(chunks + 1):
        for slot in range(1, 8):
            transfer(slot, q).wait_send()
    ahead.wait_send()


def on_device(layers, schur_blocks):
    local = schur_blocks[0]
    slab, width = local.shape
    ps = slab // 4
    depth = layers * ps
    outer = slab - ps
    sh = ps
    group = 2 * layers
    chunks = outer // ps
    merged, cousin_sum = pl.pallas_call(
        functools.partial(gather_kernel, layers),
        out_shape=(
            jax.ShapeDtypeStruct((outer, group * outer), F32),
            jax.ShapeDtypeStruct((sh, layers * sh), F32),
        ),
        in_specs=[pl.BlockSpec(memory_space=pl.ANY)],
        out_specs=(
            pl.BlockSpec(memory_space=pl.ANY),
            pl.BlockSpec(memory_space=pltpu.VMEM),
        ),
        scratch_shapes=[
            pltpu.VMEM((group, ps, depth), F32),
            pltpu.VMEM((ps, ps), F32),
            pltpu.VMEM((depth, depth), F32),
            pltpu.VMEM((ps, ps), F32),
            pltpu.VMEM((outer, depth), F32),
            pltpu.VMEM((outer, layers * outer), F32),
            pltpu.VMEM((group, outer, depth), F32),
            pltpu.VMEM((outer, depth), F32),
            pltpu.VMEM((outer, 3 * depth), BF16),
            pltpu.VMEM((layers, outer, 2 * outer), F32),
            pltpu.VMEM((sh, layers * sh), F32),
            pltpu.VMEM((sh, layers * sh), F32),
            pltpu.SemaphoreType.DMA((group, chunks + 1)),
            pltpu.SemaphoreType.DMA((group, chunks + 1)),
            pltpu.SemaphoreType.DMA((3 * layers + 1,)),
        ],
        compiler_params=pltpu.CompilerParams(
            collective_id=0, has_side_effects=True, vmem_limit_bytes=60 * 2**20
        ),
    )(local)
    return (merged[None], cousin_sum[None])


def solution(mesh):
    placed = (P("leaf", "layer", None),)
    return jax.shard_map(
        functools.partial(on_device, mesh.shape["layer"]),
        mesh=mesh,
        in_specs=placed,
        out_specs=(P("leaf", "layer", None), P("leaf", "layer", None)),
        check_vma=False,
    )
```
